32 devices in a mesh: dp: 4 (over y, x), ctx: 8 (over z, core).
Axes of the slice: x: 2, y: 2, z: 4, core: 2. Of those that a mesh axis runs over, the one named last changes fastest.
Arguments:
- inputs: bfloat16 [3, 4, 512, 1088], P(None, 'dp', 'ctx'), may hold values from -54 to 54
- lengths: int32 [3, 4, 4], P(None, 'dp'), may hold values from 1 to 509, as said below
- ln1_scale: bfloat16 [1088], P('dp'), may hold values from 0.5 to 1.5
- ln1_bias: bfloat16 [1088], P('dp'), may hold values from -4 to 4
- w_qkv: bfloat16 [1088, 3264], P('ctx', 'dp'), may hold values from -0.1875 to 0.1875
- qv_bias: bfloat16 [2176], P('dp'), may hold values from -4 to 4
- w_out: bfloat16 [1088, 1088], P('ctx', 'dp'), may hold values from -0.5 to 0.5
- out_bias: bfloat16 [1088], P('dp'), may hold values from -4 to 4
- ln2_scale: bfloat16 [1088], P('dp'), may hold values from 0.5 to 1.5
- ln2_bias: bfloat16 [1088], P('dp'), may hold values from -4 to 4
- w_up: bfloat16 [1088, 4352], P('ctx', 'dp'), may hold values from -0.1875 to 0.1875
- up_bias: bfloat16 [4352], P('dp'), may hold values from -4 to 4
- w_down: bfloat16 [4352, 1088], P('ctx', 'dp'), may hold values from -0.09375 to 0.09375
- down_bias: bfloat16 [1088], P('dp'), may hold values from -4 to 4
- out_grad: bfloat16 [3, 4, 512, 1088], P(None, 'dp', 'ctx'), may hold values from -6 to 6
Outputs:
- block_out: bfloat16 [3, 4, 512, 1088], P(None, 'dp', 'ctx')
- input_grad: bfloat16 [3, 4, 512, 1088], P(None, 'dp', 'ctx')
- ln1_scale_grad: float32 [1088], P('dp')
- ln1_bias_grad: float32 [1088], P('dp')
- w_qkv_grad: float32 [1088, 3264], P('ctx', 'dp')
- qv_bias_grad: float32 [2176], P('dp')
- w_out_grad: float32 [1088, 1088], P('ctx', 'dp')
- out_bias_grad: float32 [1088], P('dp')
- ln2_scale_grad: float32 [1088], P('dp')
- ln2_bias_grad: float32 [1088], P('dp')
- w_up_grad: float32 [1088, 4352], P('ctx', 'dp')
- up_bias_grad: float32 [4352], P('dp')
- w_down_grad: float32 [4352, 1088], P('ctx', 'dp')
- down_bias_grad: float32 [1088], P('dp')
The draws below stay inside these ranges and needn't reach their ends.
Inputs may be any that keep to these rules, and one draw needn't show every extreme that they name: The 4 lengths of each stream sum to 512.
All inputs are finite; a program needn't handle non-finite values.
Results may differ from the reference program's by a relative error of at most 0.02.
Values may be sent and summed in bfloat16 or wider, within the bound.
A program may use at most 192 MiB of HBM per device.

```python
import math
import jax
import jax.numpy as jnp
from jax import lax

D = 1088
HEADS = 17
HEAD_DIM = 64
FF = 4352
SPAN = 64
MB = 3
SEQS = 4
GROUPS = 4
STREAM = 512


def draw_inputs(key, part):
    key = jax.random.fold_in(key, 11)
    row_key, column_key, entry_key = jax.random.split(key, 3)
    full_shape = (MB, GROUPS, STREAM, D)
    row_scale = jnp.exp(jax.random.uniform(row_key, (MB, GROUPS, STREAM, 1), jnp.float32, math.log(0.3), math.log(3.0)))
    column_scale = jnp.exp(jax.random.uniform(column_key, (D,), jnp.float32, math.log(0.3), math.log(3.0)))
    entries = jnp.clip(jax.random.normal(entry_key, full_shape, jnp.float32), -6.0, 6.0)
    return (entries * row_scale * column_scale).astype(jnp.bfloat16)


def draw_lengths(key, part):
    key = jax.random.fold_in(key, 23)
    place_key, short_key, forced_key = jax.random.split(key, 3)
    cells = MB * GROUPS
    long_slot = jax.random.randint(place_key, (cells, 1), 0, SEQS)
    shorts = jax.random.randint(short_key, (cells, SEQS - 1), 1, SPAN // 4 + 1)
    forced = jax.random.randint(forced_key, (), 0, cells)
    shorts = jnp.where((jnp.arange(cells) == forced)[:, None], 1, shorts)
    longest = STREAM - jnp.sum(shorts, axis=1, keepdims=True)
    slots = jnp.arange(SEQS)[None, :]
    short_index = jnp.clip(slots - (slots > long_slot).astype(jnp.int32), 0, SEQS - 2)
    picked = jnp.take_along_axis(shorts, short_index, axis=1)
    table = jnp.where(slots == long_slot, longest, picked)
    return table.reshape(MB, GROUPS, SEQS).astype(jnp.int32)


def steps_of(rng, dims, cuts, least, largest):
    loudness = 1.0
    for axis_at, shards_of in cuts:
        draws = jax.random.uniform(jax.random.fold_in(jax.random.fold_in(rng, 6), axis_at), (shards_of,), jnp.float32, least / len(cuts), largest / len(cuts))
        loudness = loudness * jnp.repeat(jnp.exp(draws), dims[axis_at] // shards_of).reshape((-1,) + (1,) * (len(dims) - 1 - axis_at))
    return loudness


def bell_draw(stream_key, dims, scale, most, pieces=(), held_as=jnp.bfloat16):
    drawn = jax.random.normal(stream_key, dims, jnp.float32) * scale
    if len(pieces) > 0:
        drawn = steps_of(stream_key, dims, pieces, -0.22, 0.18) * drawn
    return jnp.clip(drawn, min=-most, max=most).astype(held_as)


def setup_inputs(seed: int = 0) -> dict:
    arg_keys = jax.random.split(jax.random.key(seed), 16)
    inputs = draw_inputs(jax.random.fold_in(arg_keys[15], 71), 0)
    lengths = draw_lengths(jax.random.fold_in(arg_keys[15], 71), 0)
    ln1_scale = jnp.clip(1.0 + 0.1 * jax.random.normal(arg_keys[2], (D,), jnp.float32), 0.5, 1.5).astype(jnp.bfloat16)
    ln1_bias = bell_draw(arg_keys[3], (D,), 0.3, 4.0, ((0, 4),))
    w_qkv = bell_draw(arg_keys[4], (D, 3 * D), D ** -0.5, 0.1875, ((0, 8), (1, 4)))
    qv_bias = bell_draw(arg_keys[5], (2 * D,), 0.3, 4.0, ((0, 4),))
    w_out = bell_draw(arg_keys[6], (D, D), (D // 8) ** -0.5, 0.5, ((0, 8), (1, 4)))
    out_bias = bell_draw(arg_keys[7], (D,), 0.3, 4.0, ((0, 4),))
    ln2_scale = jnp.clip(1.0 + 0.1 * jax.random.normal(arg_keys[8], (D,), jnp.float32), 0.5, 1.5).astype(jnp.bfloat16)
    ln2_bias = bell_draw(arg_keys[9], (D,), 0.3, 4.0, ((0, 4),))
    w_up = bell_draw(arg_keys[10], (D, FF), D ** -0.5, 0.1875, ((0, 8), (1, 4)))
    up_bias = bell_draw(arg_keys[11], (FF,), 0.3, 4.0, ((0, 4),))
    w_down = bell_draw(arg_keys[12], (FF, D), FF ** -0.5, 0.09375, ((0, 8), (1, 4)))
    down_bias = bell_draw(arg_keys[13], (D,), 0.3, 4.0, ((0, 4),))
    out_grad = bell_draw(arg_keys[14], (MB, GROUPS, STREAM, D), 1.0, 6.0, ((1, 4), (2, 8)))
    return dict(inputs=inputs, lengths=lengths, ln1_scale=ln1_scale, ln1_bias=ln1_bias, w_qkv=w_qkv, qv_bias=qv_bias, w_out=w_out, out_bias=out_bias, ln2_scale=ln2_scale, ln2_bias=ln2_bias, w_up=w_up, up_bias=up_bias, w_down=w_down, down_bias=down_bias, out_grad=out_grad)


@jax.custom_vjp
def low(v):
    return lax.optimization_barrier(v.astype(jnp.bfloat16)).astype(jnp.float32)

@jax.custom_vjp
def low_back(v):
    return v

def low_keep(v):
    return (low(v), None)

def low_pass(kept, grad):
    return (grad,)

def back_keep(v):
    return (v, None)

def back_low(kept, grad):
    return (low(grad),)
low.defvjp(low_keep, low_pass)
low_back.defvjp(back_keep, back_low)
EPSILON = 1e-05
SCALE = 0.125
NEGATIVE = -1e+30

def layer_norm(values, scale, shift):
    row_mean = lax.optimization_barrier(jnp.mean(values, axis=-1, keepdims=True))
    centered = values - row_mean
    variance = lax.optimization_barrier(jnp.mean(centered * centered, axis=-1, keepdims=True))
    return centered * lax.rsqrt(variance + EPSILON) * scale + shift

def matmul(left, right):
    return jnp.dot(left, right, precision=lax.Precision.HIGHEST)

def stream_block(tokens, seq_lengths, params):
    ln1_scale, ln1_bias, w_qkv, qv_bias, w_out, out_bias, ln2_scale, ln2_bias, w_up, up_bias, w_down, down_bias = params
    stream_len, model_width = tokens.shape
    positions = jnp.arange(stream_len, dtype=jnp.int32)
    seq_ends = jnp.cumsum(seq_lengths).astype(jnp.int32)
    doc_ids = lax.optimization_barrier(jnp.sum((positions[:, None] >= seq_ends[None, :]).astype(jnp.int32), axis=1))
    visible = (doc_ids[:, None] == doc_ids[None, :]) & (positions[None, :] <= positions[:, None])
    normed1 = low(layer_norm(tokens, ln1_scale, ln1_bias))
    qkv_bias = jnp.concatenate([qv_bias[:model_width], jnp.zeros_like(qv_bias[:model_width]), qv_bias[model_width:]])
    qkv = low_back(low(matmul(normed1, w_qkv) + qkv_bias))
    queries = qkv[:, :model_width].reshape(stream_len, HEADS, HEAD_DIM)
    key_heads = qkv[:, model_width:2 * model_width].reshape(stream_len, HEADS, HEAD_DIM)
    value_heads = qkv[:, 2 * model_width:].reshape(stream_len, HEADS, HEAD_DIM)
    scores = low_back(jnp.einsum('qhd,khd->hqk', queries, key_heads, precision=lax.Precision.HIGHEST) * SCALE)
    scores = jnp.where(visible[None], scores, NEGATIVE)
    weights = low(jax.nn.softmax(scores, axis=-1))
    attended = jnp.einsum('hqk,khd->qhd', weights, value_heads, precision=lax.Precision.HIGHEST)
    attended = low_back(low(attended.reshape(stream_len, model_width)))
    residual = tokens + low_back(matmul(attended, w_out) + out_bias)
    normed2 = low(layer_norm(residual, ln2_scale, ln2_bias))
    gelu_input = low_back(matmul(normed2, w_up) + up_bias)
    hidden = low(jax.nn.gelu(gelu_input))
    return residual + low_back(matmul(hidden, w_down) + down_bias)

def reference(inputs, lengths, ln1_scale, ln1_bias, w_qkv, qv_bias, w_out, out_bias, ln2_scale, ln2_bias, w_up, up_bias, w_down, down_bias, out_grad):
    params = tuple((member.astype(jnp.float32) for member in (ln1_scale, ln1_bias, w_qkv, qv_bias, w_out, out_bias, ln2_scale, ln2_bias, w_up, up_bias, w_down, down_bias)))
    streams = inputs.astype(jnp.float32).reshape(MB * GROUPS, STREAM, D)
    seq_table = lengths.reshape(MB * GROUPS, SEQS).astype(jnp.int32)
    checked = jax.checkpoint(stream_block)

    def forward(tokens_all, weights_all):

        def one_stream(paired):
            return checked(paired[0], paired[1], weights_all)
        return lax.map(one_stream, (tokens_all, seq_table))
    outputs, pullback = jax.vjp(forward, streams, params)
    grad_tokens, grad_params = pullback(out_grad.astype(jnp.float32).reshape(MB * GROUPS, STREAM, D))
    full_shape = inputs.shape
    return (outputs.reshape(full_shape).astype(jnp.bfloat16), grad_tokens.reshape(full_shape).astype(jnp.bfloat16), grad_params[0], grad_params[1], grad_params[2], grad_params[3], grad_params[4], grad_params[5], grad_params[6], grad_params[7], grad_params[8], grad_params[9], grad_params[10], grad_params[11])
```

```python
import jax
import jax.numpy as jnp
from jax import lax
from jax.sharding import PartitionSpec as P

HEADS = 17
HEAD_DIM = 64


EPSILON = 1e-05
SCALE = 0.125
NEGATIVE = -1e30


def layer_norm(values, scale, shift):
    row_mean = jnp.mean(values, axis=-1, keepdims=True)
    centered = values - row_mean
    variance = jnp.mean(centered * centered, axis=-1, keepdims=True)
    inverse = lax.rsqrt(variance + EPSILON)
    normal = centered * inverse
    return (normal * scale + shift, normal, inverse)


def norm_back(grad_normed, normal, inverse, scale):
    scaled = grad_normed * scale
    return inverse * (
        scaled
        - jnp.mean(scaled, axis=-1, keepdims=True)
        - normal * jnp.mean(scaled * normal, axis=-1, keepdims=True)
    )


def outer_sum(left, right):
    return lax.dot_general(
        left, right, (((0,), (0,)), ((), ())), preferred_element_type=jnp.float32
    )


def back_dot(gradient, weight):
    return lax.dot_general(
        gradient, weight, (((1,), (1,)), ((), ())), preferred_element_type=jnp.float32
    )


def doc_numbers(positions, seq_ends):
    return jnp.sum((positions[None, :, None] >= seq_ends[:, None, :]).astype(jnp.int32), axis=2)


def heads_first(rows):
    devices, micro, span, columns = rows.shape
    parts = rows.reshape(devices, micro, span, columns // HEAD_DIM, HEAD_DIM)
    parts = jnp.transpose(parts, (1, 3, 0, 2, 4))
    return parts.reshape(micro, columns // HEAD_DIM, devices * span, HEAD_DIM)


def rows_first(per_head, devices):
    micro, heads, stream, _ = per_head.shape
    parts = per_head.reshape(micro, heads, devices, stream // devices, HEAD_DIM)
    parts = jnp.transpose(parts, (2, 0, 3, 1, 4))
    return parts.reshape(devices, micro, stream // devices, heads * HEAD_DIM)


def batched(left, right, left_dim, right_dim):
    return lax.dot_general(
        left,
        right,
        (((left_dim,), (right_dim,)), ((0, 1), (0, 1))),
        preferred_element_type=jnp.float32,
    )


def dot32(left, right):
    return jnp.dot(left, right, preferred_element_type=jnp.float32)


def piece_route(dp_size, ctx_size):
    return [
        (q * ctx_size + r, r * dp_size + q) for q in range(dp_size) for r in range(ctx_size)
    ]


def local(
    inputs,
    lengths,
    ln1_scale,
    ln1_bias,
    w_qkv,
    qv_bias,
    w_out,
    out_bias,
    ln2_scale,
    ln2_bias,
    w_up,
    up_bias,
    w_down,
    down_bias,
    out_grad,
):
    ctx_index = lax.axis_index("ctx")
    ctx_size = lax.axis_size("ctx")
    dp_size = lax.axis_size("dp")
    micro, _, span, width = inputs.shape
    rows = micro * span
    stream = span * ctx_size
    qkv_part = w_qkv.shape[1]
    out_part = w_out.shape[1]
    bf16 = jnp.bfloat16
    f32 = jnp.float32

    tokens32 = inputs.reshape(rows, width).astype(f32)
    grad_out = out_grad.reshape(rows, width)
    grad32 = grad_out.astype(f32)

    small = (ln1_scale, ln1_bias, qv_bias, out_bias, ln2_scale, ln2_bias, down_bias)
    small_all = lax.all_gather(jnp.concatenate(small), "dp", axis=0)
    vectors = []
    start = 0
    for member in small:
        size = member.shape[0]
        vectors.append(small_all[:, start : start + size].reshape(-1).astype(f32))
        start += size
    ln1_scale, ln1_bias, qv_bias, out_bias, ln2_scale, ln2_bias, down_bias = vectors
    qkv_all = lax.all_gather(lax.all_gather(w_qkv, "ctx", axis=0, tiled=True), "dp", axis=0)
    out_all = lax.all_gather(lax.all_gather(w_out, "ctx", axis=0, tiled=True), "dp", axis=0)
    out_full = jnp.concatenate([out_all[j] for j in range(dp_size)], axis=1)
    up_here = lax.all_gather(w_up, "ctx", axis=0, tiled=True)
    down_piece = lax.all_to_all(w_down, "dp", split_axis=0, concat_axis=1, tiled=True)
    route = piece_route(dp_size, ctx_size)
    down_piece = lax.ppermute(down_piece, ("dp", "ctx"), route)
    down_here = lax.all_gather(down_piece, "ctx", axis=0, tiled=True)
    grad_all = lax.all_gather(grad_out, "dp", axis=0, tiled=True)

    normed1, normal1, inverse1 = layer_norm(tokens32, ln1_scale, ln1_bias)
    normed1 = normed1.astype(bf16)
    qkv_bias = jnp.concatenate([qv_bias[:width], jnp.zeros((width,), f32), qv_bias[width:]])
    qkv = jnp.concatenate([dot32(normed1, qkv_all[j]) for j in range(dp_size)], axis=1)
    qkv = (qkv + qkv_bias).astype(bf16)
    kv_all = lax.all_gather(qkv[:, width:].reshape(micro, span, 2 * width), "ctx", axis=0)
    kv_heads = heads_first(kv_all)
    keys, values = kv_heads[:, :HEADS], kv_heads[:, HEADS:]
    queries = heads_first(qkv[:, :width].reshape(1, micro, span, width))
    seq_ends = jnp.cumsum(lengths[:, 0], axis=1)
    key_pos = jnp.arange(stream, dtype=jnp.int32)
    query_pos = ctx_index * span + jnp.arange(span, dtype=jnp.int32)
    key_doc = doc_numbers(key_pos, seq_ends)
    query_doc = doc_numbers(query_pos, seq_ends)
    visible = (key_doc[:, None, :] == query_doc[:, :, None]) & (
        key_pos[None, None, :] <= query_pos[None, :, None]
    )
    scores = batched(queries, keys, 3, 3) * SCALE
    scores = jnp.where(visible[:, None], scores, NEGATIVE)
    weights = jnp.exp(scores - jnp.max(scores, axis=-1, keepdims=True))
    weights = (weights / jnp.sum(weights, axis=-1, keepdims=True)).astype(bf16)
    attended_heads = batched(weights, values, 3, 2)
    attended = rows_first(attended_heads.astype(bf16), 1).reshape(rows, width)
    residual = tokens32 + dot32(attended, out_full) + out_bias
    normed2, normal2, inverse2 = layer_norm(residual, ln2_scale, ln2_bias)
    normed2_all = lax.all_gather(normed2.astype(bf16), "dp", axis=0, tiled=True)

    gelu_input = dot32(normed2_all, up_here) + up_bias.astype(f32)
    hidden, gelu_pull = jax.vjp(jax.nn.gelu, gelu_input)
    hidden = hidden.astype(bf16)
    grad_upper = gelu_pull(back_dot(grad_all, down_here))[0].astype(bf16)
    both = jnp.concatenate(
        [dot32(hidden, down_here).astype(bf16), back_dot(grad_upper, up_here).astype(bf16)], axis=1
    )
    both = lax.psum_scatter(
        both.reshape(dp_size, rows, 2 * width), "dp", scatter_dimension=0
    ).astype(f32)
    block_out = (residual + both[:, :width] + down_bias).astype(bf16)
    grad_normed2 = both[:, width:]
    up_grad = lax.psum_scatter(
        outer_sum(normed2_all, grad_upper).astype(bf16), "ctx", scatter_dimension=0, tiled=True
    ).astype(f32)
    down_grad = lax.psum_scatter(
        outer_sum(hidden, grad_all).astype(bf16), "ctx", scatter_dimension=0, tiled=True
    )
    down_grad = lax.ppermute(down_grad, ("dp", "ctx"), [(b, a) for a, b in route])
    down_grad = lax.all_to_all(
        down_grad, "dp", split_axis=1, concat_axis=0, tiled=True
    ).astype(f32)

    grad_residual = grad32 + norm_back(grad_normed2, normal2, inverse2, ln2_scale)
    grad_branch = grad_residual.astype(bf16)
    grad_attended = back_dot(grad_branch, out_full).astype(bf16)
    out_grads = jnp.stack(
        [
            outer_sum(attended, grad_branch[:, j * out_part : (j + 1) * out_part])
            for j in range(dp_size)
        ]
    ).astype(bf16)
    out_grads = lax.psum_scatter(out_grads, "dp", scatter_dimension=0)
    out_grads = out_grads.reshape(ctx_size, -1, out_part)
    out_grads = lax.psum_scatter(out_grads, "ctx", scatter_dimension=0).astype(f32)
    grad_heads = heads_first(grad_attended.reshape(1, micro, span, width))
    row_dot = jnp.sum(grad_heads.astype(f32) * attended_heads, axis=-1, keepdims=True)
    grad_weights = batched(grad_heads, values, 3, 3)
    grad_scores = (weights.astype(f32) * (grad_weights - row_dot)).astype(bf16)
    grad_queries = batched(grad_scores, keys, 3, 2) * SCALE
    grad_keys = batched(grad_scores, queries, 2, 2) * SCALE
    grad_values = batched(weights, grad_heads, 2, 2)
    grad_kv = rows_first(
        jnp.concatenate([grad_keys.astype(bf16), grad_values.astype(bf16)], axis=1), ctx_size
    )
    grad_kv = lax.psum_scatter(grad_kv, "ctx", scatter_dimension=0).reshape(rows, 2 * width)
    grad_qkv = jnp.concatenate(
        [rows_first(grad_queries.astype(bf16), 1).reshape(rows, width), grad_kv], axis=1
    )
    pieces = [grad_qkv[:, j * qkv_part : (j + 1) * qkv_part] for j in range(dp_size)]
    qkv_grads = jnp.stack([outer_sum(normed1, piece) for piece in pieces]).astype(bf16)
    qkv_grads = lax.psum_scatter(qkv_grads, "dp", scatter_dimension=0)
    qkv_grads = qkv_grads.reshape(ctx_size, -1, qkv_part)
    qkv_grads = lax.psum_scatter(qkv_grads, "ctx", scatter_dimension=0).astype(f32)
    grad_normed1 = back_dot(pieces[0], qkv_all[0])
    for j in range(1, dp_size):
        grad_normed1 = grad_normed1 + back_dot(pieces[j], qkv_all[j])
    input_grad = (grad_residual + norm_back(grad_normed1, normal1, inverse1, ln1_scale)).astype(
        bf16
    )

    qkv_sums = jnp.sum(grad_qkv.astype(f32), axis=0)
    sums = (
        jnp.sum(grad_normed1 * normal1, axis=0),
        jnp.sum(grad_normed1, axis=0),
        jnp.concatenate([qkv_sums[:width], qkv_sums[2 * width :]]),
        jnp.sum(grad_branch.astype(f32), axis=0),
        jnp.sum(grad_normed2 * normal2, axis=0),
        jnp.sum(grad_normed2, axis=0),
        jnp.sum(grad32, axis=0),
    )
    sums = jnp.concatenate([member.reshape(dp_size, -1) for member in sums], axis=1)
    sums = lax.psum_scatter(sums, "dp", scatter_dimension=0)
    up_sums = jnp.sum(grad_upper.astype(f32), axis=0)
    sums = lax.psum(jnp.concatenate([sums, up_sums]), "ctx")
    cuts = []
    start = 0
    for member in small + (up_bias,):
        cuts.append(sums[start : start + member.shape[0]])
        start += member.shape[0]
    return (
        block_out.reshape(inputs.shape),
        input_grad.reshape(inputs.shape),
        cuts[0],
        cuts[1],
        qkv_grads,
        cuts[2],
        out_grads,
        cuts[3],
        cuts[4],
        cuts[5],
        up_grad,
        cuts[7],
        down_grad,
        cuts[6],
    )


def solution(mesh):
    placed = (
        P(None, "dp", "ctx", None),
        P(None, "dp", None),
        P("dp"),
        P("dp"),
        P("ctx", "dp"),
        P("dp"),
        P("ctx", "dp"),
        P("dp"),
        P("dp"),
        P("dp"),
        P("ctx", "dp"),
        P("dp"),
        P("ctx", "dp"),
        P("dp"),
        P(None, "dp", "ctx", None),
    )
    return jax.shard_map(
        local,
        mesh=mesh,
        in_specs=placed,
        out_specs=(
            P(None, "dp", "ctx", None),
            P(None, "dp", "ctx", None),
            P("dp"),
            P("dp"),
            P("ctx", "dp"),
            P("dp"),
            P("ctx", "dp"),
            P("dp"),
            P("dp"),
            P("dp"),
            P("ctx", "dp"),
            P("dp"),
            P("ctx", "dp"),
            P("dp"),
        ),
        check_vma=False,
    )
```

```python
import jax
import jax.numpy as jnp
from jax import lax
from jax.experimental import pallas as pl
from jax.experimental.pallas import tpu as pltpu
from jax.sharding import PartitionSpec as P

HEADS = 17
HEAD_DIM = 64
PAIR = 2 * HEAD_DIM
PAIRS = (HEADS + 1) // 2


EPSILON = 1e-05
SCALE = 0.125
NEGATIVE = -1e30


def layer_norm(values, scale, shift):
    row_mean = jnp.mean(values, axis=-1, keepdims=True)
    centered = values - row_mean
    variance = jnp.mean(centered * centered, axis=-1, keepdims=True)
    inverse = lax.rsqrt(variance + EPSILON)
    normal = centered * inverse
    return (normal * scale + shift, normal, inverse)


def norm_back(grad_normed, normal, inverse, scale):
    scaled = grad_normed * scale
    return inverse * (
        scaled
        - jnp.mean(scaled, axis=-1, keepdims=True)
        - normal * jnp.mean(scaled * normal, axis=-1, keepdims=True)
    )


def outer_sum(left, right):
    return lax.dot_general(
        left, right, (((0,), (0,)), ((), ())), preferred_element_type=jnp.float32
    )


def back_dot(gradient, weight):
    return lax.dot_general(
        gradient, weight, (((1,), (1,)), ((), ())), preferred_element_type=jnp.float32
    )


def head_part(block, half):
    lane = lax.broadcasted_iota(jnp.int32, block.shape, 1)
    return jnp.where(lane // HEAD_DIM == half, block.astype(jnp.float32), 0.0).astype(block.dtype)


def joined(first, second):
    lane = lax.broadcasted_iota(jnp.int32, first.shape, 1)
    return jnp.where(lane < HEAD_DIM, first, second)


def attend_kernel(first_ref, last_ref, q_ref, kv_ref, out_ref, weights_ref):
    stream = weights_ref.shape[3]
    keys = kv_ref[:, 0, 0].reshape(stream, PAIR)
    values = kv_ref[:, 0, 1].reshape(stream, PAIR)
    key_pos = lax.broadcasted_iota(jnp.int32, (q_ref.shape[1], stream), 1)
    visible = (key_pos >= first_ref[0]) & (key_pos <= last_ref[0])
    attended = []
    for half in range(2):
        scores = back_dot(head_part(q_ref[0], half), keys) * SCALE
        scores = jnp.where(visible, scores, NEGATIVE)
        weights = jnp.exp(scores - jnp.max(scores, axis=1, keepdims=True))
        weights = weights / jnp.sum(weights, axis=1, keepdims=True)
        weights = weights.astype(jnp.bfloat16)
        weights_ref[0, half] = weights
        attended.append(dot32(weights, values))
    out_ref[0] = joined(*attended).astype(jnp.bfloat16)


def attend_back_kernel(q_ref, kv_ref, grad_ref, weights_ref, grad_q_ref, grad_kv_ref):
    stream = weights_ref.shape[3]
    keys = kv_ref[:, 0, 0].reshape(stream, PAIR)
    values = kv_ref[:, 0, 1].reshape(stream, PAIR)
    grad_q = []
    grad_k = jnp.zeros((stream, PAIR), jnp.float32)
    grad_v = jnp.zeros((stream, PAIR), jnp.float32)
    for half in range(2):
        weights = weights_ref[0, half]
        weights32 = weights.astype(jnp.float32)
        grad = head_part(grad_ref[0], half)
        grad_weights = back_dot(grad, values)
        row_dot = jnp.sum(weights32 * grad_weights, axis=1, keepdims=True)
        grad_scores = (weights32 * (grad_weights - row_dot)).astype(jnp.bfloat16)
        grad_q.append(dot32(grad_scores, keys))
        grad_k = grad_k + outer_sum(grad_scores, head_part(q_ref[0], half))
        grad_v = grad_v + outer_sum(weights, grad)
    grad_q_ref[0] = (joined(*grad_q) * SCALE).astype(jnp.bfloat16)
    block = grad_kv_ref.shape
    grad_kv_ref[:, 0, 0] = (grad_k * SCALE).astype(jnp.bfloat16).reshape(block[0], block[3], PAIR)
    grad_kv_ref[:, 0, 1] = grad_v.astype(jnp.bfloat16).reshape(block[0], block[3], PAIR)


def attention_specs(span, ctx_size):
    row = pl.BlockSpec((1, span, PAIR), lambda m, p: (m, 0, p))
    kv = pl.BlockSpec((ctx_size, 1, 2, span, PAIR), lambda m, p: (0, m, 0, 0, p))
    weights = pl.BlockSpec((1, 2, span, ctx_size * span), lambda m, p: (m, p, 0, 0))
    limit = pl.BlockSpec((1, span, 1), lambda m, p: (m, 0, 0))
    return row, kv, weights, limit


def attend(first, last, queries, kv_all):
    ctx_size, micro, _, span, padded = kv_all.shape
    row, kv, weights, limit = attention_specs(span, ctx_size)
    return pl.pallas_call(
        attend_kernel,
        grid=(micro, PAIRS),
        in_specs=[limit, limit, row, kv],
        out_specs=[row, weights],
        out_shape=[
            jax.ShapeDtypeStruct((micro, span, padded), jnp.bfloat16),
            jax.ShapeDtypeStruct((micro, 2 * PAIRS, span, ctx_size * span), jnp.bfloat16),
        ],
        compiler_params=pltpu.CompilerParams(vmem_limit_bytes=24 * 2**20),
    )(first, last, queries, kv_all)


def attend_back(queries, kv_all, grad, weights_all):
    ctx_size, micro, _, span, padded = kv_all.shape
    row, kv, weights, _ = attention_specs(span, ctx_size)
    return pl.pallas_call(
        attend_back_kernel,
        grid=(micro, PAIRS),
        in_specs=[row, kv, row, weights],
        out_specs=[row, kv],
        out_shape=[
            jax.ShapeDtypeStruct((micro, span, padded), jnp.bfloat16),
            jax.ShapeDtypeStruct(kv_all.shape, jnp.bfloat16),
        ],
        compiler_params=pltpu.CompilerParams(vmem_limit_bytes=24 * 2**20),
    )(queries, kv_all, grad, weights_all)


def padded_heads(rows, micro):
    rows = jnp.pad(rows, ((0, 0), (0, PAIRS * PAIR - rows.shape[1])))
    return rows.reshape(micro, -1, PAIRS * PAIR)


def plain_heads(rows, width):
    return rows.reshape(-1, rows.shape[-1])[:, :width]


def shared(block):
    count = lax.axis_size("dp")
    return [block] + [
        lax.ppermute(block, "dp", [(s, (s + k) % count) for s in range(count)])
        for k in range(1, count)
    ]


def returned(blocks):
    count = lax.axis_size("dp")
    total = blocks[0].astype(jnp.float32)
    for k in range(1, count):
        route = [(s, (s - k) % count) for s in range(count)]
        total = total + lax.ppermute(blocks[k], "dp", route).astype(jnp.float32)
    return total


def swapped(blocks, start, step):
    stacked = jnp.stack(blocks)
    count = len(blocks)
    return [
        lax.dynamic_index_in_dim(stacked, (start + step * j) % count, 0, keepdims=False)
        for j in range(count)
    ]


def dot32(left, right):
    return jnp.dot(left, right, preferred_element_type=jnp.float32)


def piece_route(k, dp_size, ctx_size):
    return [
        (d * ctx_size + r, r * dp_size + (d + k) % dp_size)
        for d in range(dp_size)
        for r in range(ctx_size)
    ]


def local(
    inputs,
    lengths,
    ln1_scale,
    ln1_bias,
    w_qkv,
    qv_bias,
    w_out,
    out_bias,
    ln2_scale,
    ln2_bias,
    w_up,
    up_bias,
    w_down,
    down_bias,
    out_grad,
):
    ctx_index = lax.axis_index("ctx")
    ctx_size = lax.axis_size("ctx")
    dp_index = lax.axis_index("dp")
    dp_size = lax.axis_size("dp")
    piece_index = (dp_index * ctx_size + ctx_index) % dp_size
    micro, _, span, width = inputs.shape
    rows = micro * span
    qkv_part = w_qkv.shape[1]
    out_part = w_out.shape[1]
    bf16 = jnp.bfloat16
    f32 = jnp.float32

    tokens32 = inputs.reshape(rows, width).astype(f32)
    grad_out = out_grad.reshape(rows, width)
    grad32 = grad_out.astype(f32)

    small = (ln1_scale, ln1_bias, qv_bias, out_bias, ln2_scale, ln2_bias, down_bias)
    small_all = lax.all_gather(jnp.concatenate(small), "dp", axis=0)
    vectors = []
    start = 0
    for member in small:
        size = member.shape[0]
        vectors.append(small_all[:, start : start + size].reshape(-1).astype(f32))
        start += size
    ln1_scale, ln1_bias, qv_bias, out_bias, ln2_scale, ln2_bias, down_bias = vectors
    qkv_near = shared(lax.all_gather(w_qkv, "ctx", axis=0, tiled=True))
    out_near = shared(lax.all_gather(w_out, "ctx", axis=0, tiled=True))
    grad_all = jnp.concatenate(shared(grad_out), axis=0)
    up_here = lax.all_gather(w_up, "ctx", axis=0, tiled=True)
    down_rows = w_down.reshape(dp_size, -1, out_part)
    down_piece = [
        lax.ppermute(
            lax.dynamic_index_in_dim(down_rows, (dp_index + k) % dp_size, 0, keepdims=False),
            ("dp", "ctx"),
            piece_route(k, dp_size, ctx_size),
        )
        for k in range(dp_size)
    ]
    down_piece = jnp.concatenate(swapped(down_piece, piece_index, -1), axis=1)
    down_here = lax.all_gather(down_piece, "ctx", axis=0, tiled=True)

    normed1, normal1, inverse1 = layer_norm(tokens32, ln1_scale, ln1_bias)
    normed1 = normed1.astype(bf16)
    qkv_bias = jnp.concatenate([qv_bias[:width], jnp.zeros((width,), f32), qv_bias[width:]])
    qkv = swapped([dot32(normed1, piece) for piece in qkv_near], dp_index, -1)
    qkv = jnp.concatenate(qkv, axis=1)
    qkv = (qkv + qkv_bias).astype(bf16)
    queries = padded_heads(qkv[:, :width], micro)
    keys = padded_heads(qkv[:, width : 2 * width], micro)
    values = padded_heads(qkv[:, 2 * width :], micro)
    kv_all = lax.all_gather(jnp.stack([keys, values], axis=1), "ctx", axis=0)
    seq_ends = jnp.cumsum(lengths[:, 0], axis=1)
    last = ctx_index * span + jnp.arange(span, dtype=jnp.int32)
    last = jnp.broadcast_to(last[None, :, None], (micro, span, 1))
    ends = seq_ends[:, None, :]
    first = jnp.max(jnp.where(ends <= last, ends, 0), axis=2, keepdims=True).astype(jnp.int32)
    attended, weights = attend(first, last, queries, kv_all)
    attended = plain_heads(attended, width)
    branch = swapped([dot32(attended, piece) for piece in out_near], dp_index, -1)
    residual = tokens32 + jnp.concatenate(branch, axis=1) + out_bias
    normed2, normal2, inverse2 = layer_norm(residual, ln2_scale, ln2_bias)
    normed2_all = jnp.concatenate(shared(normed2.astype(bf16)), axis=0)

    gelu_input = dot32(normed2_all, up_here) + up_bias.astype(f32)
    hidden, gelu_pull = jax.vjp(jax.nn.gelu, gelu_input)
    hidden = hidden.astype(bf16)
    grad_upper = gelu_pull(back_dot(grad_all, down_here))[0].astype(bf16)
    both = jnp.concatenate(
        [dot32(hidden, down_here).astype(bf16), back_dot(grad_upper, up_here).astype(bf16)], axis=1
    )
    both = returned([both[k * rows : (k + 1) * rows] for k in range(dp_size)])
    block_out = (residual + both[:, :width] + down_bias).astype(bf16)
    grad_normed2 = both[:, width:]
    up_grad = lax.psum_scatter(
        outer_sum(normed2_all, grad_upper).astype(bf16).reshape(ctx_size, -1, up_here.shape[1]),
        "ctx",
        scatter_dimension=0,
    ).astype(f32)
    down_grad = lax.psum_scatter(
        outer_sum(hidden, grad_all).astype(bf16).reshape(ctx_size, -1, width),
        "ctx",
        scatter_dimension=0,
    )
    down_cols = [down_grad[:, j * out_part : (j + 1) * out_part] for j in range(dp_size)]
    down_cols = swapped(down_cols, piece_index, -1)
    down_grad = [
        lax.ppermute(
            down_cols[k], ("dp", "ctx"), [(b, a) for a, b in piece_route(k, dp_size, ctx_size)]
        )
        for k in range(dp_size)
    ]
    down_grad = jnp.concatenate(swapped(down_grad, -dp_index, 1), axis=0).astype(f32)

    grad_residual = grad32 + norm_back(grad_normed2, normal2, inverse2, ln2_scale)
    grad_branch = grad_residual.astype(bf16)
    branch_parts = [
        grad_branch[:, j * out_part : (j + 1) * out_part] for j in range(dp_size)
    ]
    branch_parts = swapped(branch_parts, dp_index, -1)
    grad_attended = back_dot(branch_parts[0], out_near[0])
    for k in range(1, dp_size):
        grad_attended = grad_attended + back_dot(branch_parts[k], out_near[k])
    grad_attended = padded_heads(grad_attended.astype(bf16), micro)
    out_grads = returned([outer_sum(attended, part).astype(bf16) for part in branch_parts])
    out_grads = out_grads.astype(bf16)
    out_grads = out_grads.reshape(ctx_size, -1, out_part)
    out_grads = lax.psum_scatter(out_grads, "ctx", scatter_dimension=0).astype(f32)
    grad_queries, grad_kv = attend_back(queries, kv_all, grad_attended, weights)
    grad_kv = lax.psum_scatter(grad_kv, "ctx", scatter_dimension=0)
    grad_qkv = jnp.concatenate(
        [
            plain_heads(grad_queries, width),
            plain_heads(grad_kv[:, 0], width),
            plain_heads(grad_kv[:, 1], width),
        ],
        axis=1,
    )
    pieces = [grad_qkv[:, j * qkv_part : (j + 1) * qkv_part] for j in range(dp_size)]
    pieces = swapped(pieces, dp_index, -1)
    qkv_grads = returned([outer_sum(normed1, piece).astype(bf16) for piece in pieces])
    grad_normed1 = back_dot(pieces[0], qkv_near[0])
    for j in range(1, dp_size):
        grad_normed1 = grad_normed1 + back_dot(pieces[j], qkv_near[j])
    input_grad = (grad_residual + norm_back(grad_normed1, normal1, inverse1, ln1_scale)).astype(
        bf16
    )

    qkv_sums = jnp.sum(grad_qkv.astype(f32), axis=0)
    sums = (
        jnp.sum(grad_normed1 * normal1, axis=0),
        jnp.sum(grad_normed1, axis=0),
        jnp.concatenate([qkv_sums[:width], qkv_sums[2 * width :]]),
        jnp.sum(grad_branch.astype(f32), axis=0),
        jnp.sum(grad_normed2 * normal2, axis=0),
        jnp.sum(grad_normed2, axis=0),
        jnp.sum(grad32, axis=0),
    )
    sums = jnp.concatenate([member.reshape(dp_size, -1) for member in sums], axis=1)
    sums = returned(swapped([sums[j] for j in range(dp_size)], dp_index, -1))
    up_sums = jnp.sum(grad_upper.astype(f32), axis=0)
    sums = jnp.concatenate([sums, up_sums]).reshape(-1, qkv_part)
    sums = jnp.pad(sums, ((0, 8 - sums.shape[0]), (0, 0)))
    sums = jnp.broadcast_to(sums[None], (ctx_size,) + sums.shape)
    qkv_rows = width // ctx_size
    qkv_grads = jnp.concatenate([qkv_grads.reshape(ctx_size, qkv_rows, qkv_part), sums], axis=1)
    qkv_grads = lax.psum_scatter(qkv_grads.astype(bf16), "ctx", scatter_dimension=0).astype(f32)
    sums = qkv_grads[qkv_rows:].reshape(-1)
    qkv_grads = qkv_grads[:qkv_rows]
    cuts = []
    start = 0
    for member in small + (up_bias,):
        cuts.append(sums[start : start + member.shape[0]])
        start += member.shape[0]
    return (
        block_out.reshape(inputs.shape),
        input_grad.reshape(inputs.shape),
        cuts[0],
        cuts[1],
        qkv_grads,
        cuts[2],
        out_grads,
        cuts[3],
        cuts[4],
        cuts[5],
        up_grad,
        cuts[7],
        down_grad,
        cuts[6],
    )


def solution(mesh):
    placed = (
        P(None, "dp", "ctx", None),
        P(None, "dp", None),
        P("dp"),
        P("dp"),
        P("ctx", "dp"),
        P("dp"),
        P("ctx", "dp"),
        P("dp"),
        P("dp"),
        P("dp"),
        P("ctx", "dp"),
        P("dp"),
        P("ctx", "dp"),
        P("dp"),
        P(None, "dp", "ctx", None),
    )
    return jax.shard_map(
        local,
        mesh=mesh,
        in_specs=placed,
        out_specs=(
            P(None, "dp", "ctx", None),
            P(None, "dp", "ctx", None),
            P("dp"),
            P("dp"),
            P("ctx", "dp"),
            P("dp"),
            P("ctx", "dp"),
            P("dp"),
            P("dp"),
            P("dp"),
            P("ctx", "dp"),
            P("dp"),
            P("ctx", "dp"),
            P("dp"),
        ),
        check_vma=False,
    )
```

```python
import jax
import jax.numpy as jnp
from jax import lax
from jax.experimental import pallas as pl
from jax.experimental.pallas import tpu as pltpu
from jax.sharding import PartitionSpec as P

HEADS = 17
HEAD_DIM = 64
PAIR = 2 * HEAD_DIM
PAIRS = (HEADS + 1) // 2
AT_ONCE = 3


EPSILON = 1e-05
SCALE = 0.125
NEGATIVE = -1e30


def layer_norm(values, scale, shift):
    row_mean = jnp.mean(values, axis=-1, keepdims=True)
    centered = values - row_mean
    variance = jnp.mean(centered * centered, axis=-1, keepdims=True)
    inverse = lax.rsqrt(variance + EPSILON)
    normal = centered * inverse
    return (normal * scale + shift, normal, inverse)


def norm_back(grad_normed, normal, inverse, scale):
    scaled = grad_normed * scale
    return inverse * (
        scaled
        - jnp.mean(scaled, axis=-1, keepdims=True)
        - normal * jnp.mean(scaled * normal, axis=-1, keepdims=True)
    )


def outer_sum(left, right):
    return lax.dot_general(
        left, right, (((0,), (0,)), ((), ())), preferred_element_type=jnp.float32
    )


def back_dot(gradient, weight):
    return lax.dot_general(
        gradient, weight, (((1,), (1,)), ((), ())), preferred_element_type=jnp.float32
    )


def head_part(block, half):
    lane = lax.broadcasted_iota(jnp.int32, block.shape, 1)
    return jnp.where(lane // HEAD_DIM == half, block.astype(jnp.float32), 0.0).astype(block.dtype)


def joined(first, second):
    lane = lax.broadcasted_iota(jnp.int32, first.shape, 1)
    return jnp.where(lane < HEAD_DIM, first, second)


def attend_kernel(first_ref, last_ref, q_ref, kv_ref, out_ref, weights_ref):
    stream = weights_ref.shape[3]
    key_pos = lax.broadcasted_iota(jnp.int32, (q_ref.shape[1], stream), 1)
    visible = (key_pos >= first_ref[0]) & (key_pos <= last_ref[0])
    for pair in range(AT_ONCE):
        lanes = slice(pair * PAIR, (pair + 1) * PAIR)
        keys = kv_ref[:, 0, 0, :, lanes].reshape(stream, PAIR)
        values = kv_ref[:, 0, 1, :, lanes].reshape(stream, PAIR)
        queries = q_ref[0, :, lanes]
        attended = []
        for half in range(2):
            scores = back_dot(head_part(queries, half), keys) * SCALE
            scores = jnp.where(visible, scores, NEGATIVE)
            weights = jnp.exp(scores - jnp.max(scores, axis=1, keepdims=True))
            weights = weights / jnp.sum(weights, axis=1, keepdims=True)
            weights = weights.astype(jnp.bfloat16)
            weights_ref[0, 2 * pair + half] = weights
            attended.append(dot32(weights, values))
        out_ref[0, :, lanes] = joined(*attended).astype(jnp.bfloat16)


def attend_back_kernel(q_ref, kv_ref, grad_ref, weights_ref, grad_q_ref, grad_kv_ref):
    stream = weights_ref.shape[3]
    block = grad_kv_ref.shape
    shape = (block[0], block[3], PAIR)
    for pair in range(AT_ONCE):
        lanes = slice(pair * PAIR, (pair + 1) * PAIR)
        keys = kv_ref[:, 0, 0, :, lanes].reshape(stream, PAIR)
        values = kv_ref[:, 0, 1, :, lanes].reshape(stream, PAIR)
        grad_q = []
        grad_k = jnp.zeros((stream, PAIR), jnp.float32)
        grad_v = jnp.zeros((stream, PAIR), jnp.float32)
        for half in range(2):
            weights = weights_ref[0, 2 * pair + half]
            weights32 = weights.astype(jnp.float32)
            grad = head_part(grad_ref[0, :, lanes], half)
            grad_weights = back_dot(grad, values)
            row_dot = jnp.sum(weights32 * grad_weights, axis=1, keepdims=True)
            grad_scores = (weights32 * (grad_weights - row_dot)).astype(jnp.bfloat16)
            grad_q.append(dot32(grad_scores, keys))
            grad_k = grad_k + outer_sum(grad_scores, head_part(q_ref[0, :, lanes], half))
            grad_v = grad_v + outer_sum(weights, grad)
        grad_q_ref[0, :, lanes] = (joined(*grad_q) * SCALE).astype(jnp.bfloat16)
        grad_kv_ref[:, 0, 0, :, lanes] = (grad_k * SCALE).astype(jnp.bfloat16).reshape(shape)
        grad_kv_ref[:, 0, 1, :, lanes] = grad_v.astype(jnp.bfloat16).reshape(shape)


def attention_specs(span, ctx_size):
    row = pl.BlockSpec((1, span, AT_ONCE * PAIR), lambda m, p: (m, 0, p))
    kv = pl.BlockSpec((ctx_size, 1, 2, span, AT_ONCE * PAIR), lambda m, p: (0, m, 0, 0, p))
    weights = pl.BlockSpec((1, 2 * AT_ONCE, span, ctx_size * span), lambda m, p: (m, p, 0, 0))
    limit = pl.BlockSpec((1, span, 1), lambda m, p: (m, 0, 0))
    return row, kv, weights, limit


def attend(first, last, queries, kv_all):
    ctx_size, micro, _, span, padded = kv_all.shape
    row, kv, weights, limit = attention_specs(span, ctx_size)
    return pl.pallas_call(
        attend_kernel,
        grid=(micro, PAIRS // AT_ONCE),
        in_specs=[limit, limit, row, kv],
        out_specs=[row, weights],
        out_shape=[
            jax.ShapeDtypeStruct((micro, span, padded), jnp.bfloat16),
            jax.ShapeDtypeStruct((micro, 2 * PAIRS, span, ctx_size * span), jnp.bfloat16),
        ],
        compiler_params=pltpu.CompilerParams(vmem_limit_bytes=24 * 2**20),
    )(first, last, queries, kv_all)


def attend_back(queries, kv_all, grad, weights_all):
    ctx_size, micro, _, span, padded = kv_all.shape
    row, kv, weights, _ = attention_specs(span, ctx_size)
    return pl.pallas_call(
        attend_back_kernel,
        grid=(micro, PAIRS // AT_ONCE),
        in_specs=[row, kv, row, weights],
        out_specs=[row, kv],
        out_shape=[
            jax.ShapeDtypeStruct((micro, span, padded), jnp.bfloat16),
            jax.ShapeDtypeStruct(kv_all.shape, jnp.bfloat16),
        ],
        compiler_params=pltpu.CompilerParams(vmem_limit_bytes=24 * 2**20),
    )(queries, kv_all, grad, weights_all)


def padded_heads(rows, micro):
    rows = jnp.pad(rows, ((0, 0), (0, PAIRS * PAIR - rows.shape[1])))
    return rows.reshape(micro, -1, PAIRS * PAIR)


def plain_heads(rows, width):
    return rows.reshape(-1, rows.shape[-1])[:, :width]


def shared(block):
    count = lax.axis_size("dp")
    return [block] + [
        lax.ppermute(block, "dp", [(s, (s + k) % count) for s in range(count)])
        for k in range(1, count)
    ]


def returned(blocks):
    count = lax.axis_size("dp")
    total = blocks[0].astype(jnp.float32)
    for k in range(1, count):
        route = [(s, (s - k) % count) for s in range(count)]
        total = total + lax.ppermute(blocks[k], "dp", route).astype(jnp.float32)
    return total


def swapped(blocks, start, step):
    stacked = jnp.stack(blocks)
    count = len(blocks)
    return [
        lax.dynamic_index_in_dim(stacked, (start + step * j) % count, 0, keepdims=False)
        for j in range(count)
    ]


def dot32(left, right):
    return jnp.dot(left, right, preferred_element_type=jnp.float32)


def piece_route(k, dp_size, ctx_size):
    return [
        (d * ctx_size + r, r * dp_size + (d + k) % dp_size)
        for d in range(dp_size)
        for r in range(ctx_size)
    ]


def local(
    inputs,
    lengths,
    ln1_scale,
    ln1_bias,
    w_qkv,
    qv_bias,
    w_out,
    out_bias,
    ln2_scale,
    ln2_bias,
    w_up,
    up_bias,
    w_down,
    down_bias,
    out_grad,
):
    ctx_index = lax.axis_index("ctx")
    ctx_size = lax.axis_size("ctx")
    dp_index = lax.axis_index("dp")
    dp_size = lax.axis_size("dp")
    piece_index = (dp_index * ctx_size + ctx_index) % dp_size
    micro, _, span, width = inputs.shape
    rows = micro * span
    qkv_part = w_qkv.shape[1]
    out_part = w_out.shape[1]
    bf16 = jnp.bfloat16
    f32 = jnp.float32

    tokens32 = inputs.reshape(rows, width).astype(f32)
    grad_out = out_grad.reshape(rows, width)
    grad32 = grad_out.astype(f32)

    small = (ln1_scale, ln1_bias, qv_bias, out_bias, ln2_scale, ln2_bias, down_bias)
    small_all = lax.all_gather(jnp.concatenate(small), "dp", axis=0)
    vectors = []
    start = 0
    for member in small:
        size = member.shape[0]
        vectors.append(small_all[:, start : start + size].reshape(-1).astype(f32))
        start += size
    ln1_scale, ln1_bias, qv_bias, out_bias, ln2_scale, ln2_bias, down_bias = vectors
    lead = qkv_part // 256 * 128 or qkv_part // 2
    rest = qkv_part - lead
    lead_rows = lax.all_gather(w_qkv[:, :lead], "ctx", axis=0, tiled=True)
    rest_rows = jnp.concatenate(shared(w_qkv[:, lead:]), axis=1)
    lead_rows, rest_rows = lax.optimization_barrier((lead_rows, rest_rows))
    rest_near = lax.all_gather(rest_rows, "ctx", axis=0, tiled=True)
    lead_near = shared(lead_rows)
    out_near = shared(lax.all_gather(w_out, "ctx", axis=0, tiled=True))
    grad_all = jnp.concatenate(shared(grad_out), axis=0)
    up_here = lax.all_gather(w_up, "ctx", axis=0, tiled=True)
    down_rows = w_down.reshape(dp_size, -1, out_part)
    down_piece = [
        lax.ppermute(
            lax.dynamic_index_in_dim(down_rows, (dp_index + k) % dp_size, 0, keepdims=False),
            ("dp", "ctx"),
            piece_route(k, dp_size, ctx_size),
        )
        for k in range(dp_size)
    ]
    down_piece = jnp.concatenate(swapped(down_piece, piece_index, -1), axis=1)
    down_here = lax.all_gather(down_piece, "ctx", axis=0, tiled=True)

    normed1, normal1, inverse1 = layer_norm(tokens32, ln1_scale, ln1_bias)
    normed1 = normed1.astype(bf16)
    qkv_bias = jnp.concatenate([qv_bias[:width], jnp.zeros((width,), f32), qv_bias[width:]])
    rest_qkv = dot32(normed1, rest_near)
    qkv = [
        jnp.concatenate(
            [dot32(normed1, lead_near[k]), rest_qkv[:, k * rest : (k + 1) * rest]], axis=1
        )
        for k in range(dp_size)
    ]
    qkv = swapped(qkv, dp_index, -1)
    qkv = jnp.concatenate(qkv, axis=1)
    qkv = (qkv + qkv_bias).astype(bf16)
    queries = padded_heads(qkv[:, :width], micro)
    keys = padded_heads(qkv[:, width : 2 * width], micro)
    values = padded_heads(qkv[:, 2 * width :], micro)
    kv_all = lax.all_gather(jnp.stack([keys, values], axis=1), "ctx", axis=0)
    seq_ends = jnp.cumsum(lengths[:, 0], axis=1)
    last = ctx_index * span + jnp.arange(span, dtype=jnp.int32)
    last = jnp.broadcast_to(last[None, :, None], (micro, span, 1))
    ends = seq_ends[:, None, :]
    first = jnp.max(jnp.where(ends <= last, ends, 0), axis=2, keepdims=True).astype(jnp.int32)
    attended, weights = attend(first, last, queries, kv_all)
    attended = plain_heads(attended, width)
    branch = swapped([dot32(attended, piece) for piece in out_near], dp_index, -1)
    residual = tokens32 + jnp.concatenate(branch, axis=1) + out_bias
    normed2, normal2, inverse2 = layer_norm(residual, ln2_scale, ln2_bias)
    normed2_all = jnp.concatenate(shared(normed2.astype(bf16)), axis=0)

    gelu_input = dot32(normed2_all, up_here) + up_bias.astype(f32)
    hidden, gelu_pull = jax.vjp(jax.nn.gelu, gelu_input)
    hidden = hidden.astype(bf16)
    grad_upper = gelu_pull(back_dot(grad_all, down_here))[0].astype(bf16)
    both = jnp.concatenate(
        [dot32(hidden, down_here).astype(bf16), back_dot(grad_upper, up_here).astype(bf16)], axis=1
    )
    both = returned([both[k * rows : (k + 1) * rows] for k in range(dp_size)])
    up_grad = outer_sum(normed2_all, grad_upper).astype(bf16)
    down_grad = outer_sum(hidden, grad_all).astype(bf16)
    both, up_grad, down_grad = lax.optimization_barrier((both, up_grad, down_grad))
    block_out = (residual + both[:, :width] + down_bias).astype(bf16)
    grad_normed2 = both[:, width:]
    up_grad = lax.psum_scatter(up_grad.reshape(ctx_size, -1, up_here.shape[1]), "ctx")
    down_grad = lax.psum_scatter(down_grad.reshape(ctx_size, -1, width), "ctx")
    kept_down = down_grad
    down_cols = [down_grad[:, j * out_part : (j + 1) * out_part] for j in range(dp_size)]
    down_cols = swapped(down_cols, piece_index, -1)
    down_grad = [
        lax.ppermute(
            down_cols[k], ("dp", "ctx"), [(b, a) for a, b in piece_route(k, dp_size, ctx_size)]
        )
        for k in range(dp_size)
    ]
    down_grad = jnp.concatenate(swapped(down_grad, -dp_index, 1), axis=0).astype(f32)

    grad_residual = grad32 + norm_back(grad_normed2, normal2, inverse2, ln2_scale)
    grad_branch = grad_residual.astype(bf16)
    branch_parts = [
        grad_branch[:, j * out_part : (j + 1) * out_part] for j in range(dp_size)
    ]
    branch_parts = swapped(branch_parts, dp_index, -1)
    grad_attended = back_dot(branch_parts[0], out_near[0])
    for k in range(1, dp_size):
        grad_attended = grad_attended + back_dot(branch_parts[k], out_near[k])
    grad_attended = padded_heads(grad_attended.astype(bf16), micro)
    out_grads = outer_sum(attended, jnp.concatenate(branch_parts, axis=1)).astype(bf16)
    out_grads = lax.psum_scatter(out_grads.reshape(ctx_size, -1, width), "ctx")
    grad_queries, grad_kv = attend_back(queries, kv_all, grad_attended, weights)
    grad_kv, up_grad, kept_down, out_grads = lax.optimization_barrier(
        (grad_kv, up_grad, kept_down, out_grads)
    )
    up_grad = up_grad.astype(f32)
    out_grads = returned(
        [out_grads[:, k * out_part : (k + 1) * out_part] for k in range(dp_size)]
    )
    grad_kv = lax.psum_scatter(grad_kv, "ctx", scatter_dimension=0)
    grad_qkv = jnp.concatenate(
        [
            plain_heads(grad_queries, width),
            plain_heads(grad_kv[:, 0], width),
            plain_heads(grad_kv[:, 1], width),
        ],
        axis=1,
    )
    pieces = [grad_qkv[:, j * qkv_part : (j + 1) * qkv_part] for j in range(dp_size)]
    pieces = swapped(pieces, dp_index, -1)
    lead_pieces = [piece[:, :lead] for piece in pieces]
    rest_pieces = jnp.concatenate([piece[:, lead:] for piece in pieces], axis=1)
    rest_grads = outer_sum(normed1, rest_pieces).astype(bf16)
    rest_grads = lax.psum_scatter(rest_grads.reshape(ctx_size, -1, dp_size * rest), "ctx")
    rest_grads = returned([rest_grads[:, k * rest : (k + 1) * rest] for k in range(dp_size)])
    lead_grads = returned([outer_sum(normed1, piece).astype(bf16) for piece in lead_pieces])
    grad_normed1 = back_dot(rest_pieces, rest_near)
    for k in range(dp_size):
        grad_normed1 = grad_normed1 + back_dot(lead_pieces[k], lead_near[k])
    input_grad = (grad_residual + norm_back(grad_normed1, normal1, inverse1, ln1_scale)).astype(
        bf16
    )

    qkv_sums = jnp.sum(grad_qkv.astype(f32), axis=0)
    sums = (
        jnp.sum(grad_normed1 * normal1, axis=0),
        jnp.sum(grad_normed1, axis=0),
        jnp.concatenate([qkv_sums[:width], qkv_sums[2 * width :]]),
        jnp.sum(grad_branch.astype(f32), axis=0),
        jnp.sum(grad_normed2 * normal2, axis=0),
        jnp.sum(grad_normed2, axis=0),
        jnp.sum(grad32, axis=0),
    )
    sums = jnp.concatenate([member.reshape(dp_size, -1) for member in sums], axis=1)
    sums = returned(swapped([sums[j] for j in range(dp_size)], dp_index, -1))
    up_sums = jnp.sum(grad_upper.astype(f32), axis=0)
    sums = jnp.concatenate([sums, up_sums])
    sum_rows = -(-sums.shape[0] // (8 * lead)) * 8
    sums = jnp.pad(sums, (0, sum_rows * lead - sums.shape[0])).reshape(1, sum_rows, lead)
    sums = jnp.broadcast_to(sums, (ctx_size, sum_rows, lead))
    qkv_rows = width // ctx_size
    lead_grads = jnp.concatenate([lead_grads.reshape(ctx_size, qkv_rows, lead), sums], axis=1)
    lead_grads = lax.psum_scatter(lead_grads.astype(bf16), "ctx").astype(f32)
    sums = lead_grads[qkv_rows:].reshape(-1)
    qkv_grads = jnp.concatenate([lead_grads[:qkv_rows], rest_grads], axis=1)
    cuts = []
    start = 0
    for member in small + (up_bias,):
        cuts.append(sums[start : start + member.shape[0]])
        start += member.shape[0]
    return (
        block_out.reshape(inputs.shape),
        input_grad.reshape(inputs.shape),
        cuts[0],
        cuts[1],
        qkv_grads,
        cuts[2],
        out_grads,
        cuts[3],
        cuts[4],
        cuts[5],
        up_grad,
        cuts[7],
        down_grad,
        cuts[6],
    )


def solution(mesh):
    placed = (
        P(None, "dp", "ctx", None),
        P(None, "dp", None),
        P("dp"),
        P("dp"),
        P("ctx", "dp"),
        P("dp"),
        P("ctx", "dp"),
        P("dp"),
        P("dp"),
        P("dp"),
        P("ctx", "dp"),
        P("dp"),
        P("ctx", "dp"),
        P("dp"),
        P(None, "dp", "ctx", None),
    )
    return jax.shard_map(
        local,
        mesh=mesh,
        in_specs=placed,
        out_specs=(
            P(None, "dp", "ctx", None),
            P(None, "dp", "ctx", None),
            P("dp"),
            P("dp"),
            P("ctx", "dp"),
            P("dp"),
            P("ctx", "dp"),
            P("dp"),
            P("dp"),
            P("dp"),
            P("ctx", "dp"),
            P("dp"),
            P("ctx", "dp"),
            P("dp"),
        ),
        check_vma=False,
    )
```

```python
import jax
import jax.numpy as jnp
from jax import lax
from jax.experimental import pallas as pl
from jax.experimental.pallas import tpu as pltpu
from jax.sharding import PartitionSpec as P

HEADS = 17
HEAD_DIM = 64
PAIR = 2 * HEAD_DIM
PAIRS = (HEADS + 1) // 2
AT_ONCE = 3


EPSILON = 1e-05
SCALE = 0.125
NEGATIVE = -1e30


def layer_norm(values, scale, shift):
    row_mean = jnp.mean(values, axis=-1, keepdims=True)
    centered = values - row_mean
    variance = jnp.mean(centered * centered, axis=-1, keepdims=True)
    inverse = lax.rsqrt(variance + EPSILON)
    normal = centered * inverse
    return (normal * scale + shift, normal, inverse)


def norm_back(grad_normed, normal, inverse, scale):
    scaled = grad_normed * scale
    return inverse * (
        scaled
        - jnp.mean(scaled, axis=-1, keepdims=True)
        - normal * jnp.mean(scaled * normal, axis=-1, keepdims=True)
    )


def outer_sum(left, right):
    return lax.dot_general(
        left, right, (((0,), (0,)), ((), ())), preferred_element_type=jnp.float32
    )


def back_dot(gradient, weight):
    return lax.dot_general(
        gradient, weight, (((1,), (1,)), ((), ())), preferred_element_type=jnp.float32
    )


def head_part(block, half):
    lane = lax.broadcasted_iota(jnp.int32, block.shape, 1)
    return jnp.where(lane // HEAD_DIM == half, block.astype(jnp.float32), 0.0).astype(block.dtype)


def joined(first, second):
    lane = lax.broadcasted_iota(jnp.int32, first.shape, 1)
    return jnp.where(lane < HEAD_DIM, first, second)


def attend_kernel(first_ref, last_ref, q_ref, kv_ref, out_ref, weights_ref):
    stream = weights_ref.shape[3]
    key_pos = lax.broadcasted_iota(jnp.int32, (q_ref.shape[1], stream), 1)
    visible = (key_pos >= first_ref[0]) & (key_pos <= last_ref[0])
    for pair in range(AT_ONCE):
        lanes = slice(pair * PAIR, (pair + 1) * PAIR)
        keys = kv_ref[:, 0, 0, :, lanes].reshape(stream, PAIR)
        values = kv_ref[:, 0, 1, :, lanes].reshape(stream, PAIR)
        queries = q_ref[0, :, lanes]
        attended = []
        for half in range(2):
            scores = back_dot(head_part(queries, half), keys) * SCALE
            scores = jnp.where(visible, scores, NEGATIVE)
            weights = jnp.exp(scores - jnp.max(scores, axis=1, keepdims=True))
            weights = weights / jnp.sum(weights, axis=1, keepdims=True)
            weights = weights.astype(jnp.bfloat16)
            weights_ref[0, 2 * pair + half] = weights
            attended.append(dot32(weights, values))
        out_ref[0, :, lanes] = joined(*attended).astype(jnp.bfloat16)


def attend_back_kernel(q_ref, kv_ref, grad_ref, weights_ref, grad_q_ref, grad_kv_ref):
    stream = weights_ref.shape[3]
    block = grad_kv_ref.shape
    shape = (block[0], block[3], PAIR)
    for pair in range(AT_ONCE):
        lanes = slice(pair * PAIR, (pair + 1) * PAIR)
        keys = kv_ref[:, 0, 0, :, lanes].reshape(stream, PAIR)
        values = kv_ref[:, 0, 1, :, lanes].reshape(stream, PAIR)
        grad_q = []
        grad_k = jnp.zeros((stream, PAIR), jnp.float32)
        grad_v = jnp.zeros((stream, PAIR), jnp.float32)
        for half in range(2):
            weights = weights_ref[0, 2 * pair + half]
            weights32 = weights.astype(jnp.float32)
            grad = head_part(grad_ref[0, :, lanes], half)
            grad_weights = back_dot(grad, values)
            row_dot = jnp.sum(weights32 * grad_weights, axis=1, keepdims=True)
            grad_scores = (weights32 * (grad_weights - row_dot)).astype(jnp.bfloat16)
            grad_q.append(dot32(grad_scores, keys))
            grad_k = grad_k + outer_sum(grad_scores, head_part(q_ref[0, :, lanes], half))
            grad_v = grad_v + outer_sum(weights, grad)
        grad_q_ref[0, :, lanes] = (joined(*grad_q) * SCALE).astype(jnp.bfloat16)
        grad_kv_ref[:, 0, 0, :, lanes] = (grad_k * SCALE).astype(jnp.bfloat16).reshape(shape)
        grad_kv_ref[:, 0, 1, :, lanes] = grad_v.astype(jnp.bfloat16).reshape(shape)


def attention_specs(span, ctx_size):
    row = pl.BlockSpec((1, span, AT_ONCE * PAIR), lambda m, p: (m, 0, p))
    kv = pl.BlockSpec((ctx_size, 1, 2, span, AT_ONCE * PAIR), lambda m, p: (0, m, 0, 0, p))
    weights = pl.BlockSpec((1, 2 * AT_ONCE, span, ctx_size * span), lambda m, p: (m, p, 0, 0))
    limit = pl.BlockSpec((1, span, 1), lambda m, p: (m, 0, 0))
    return row, kv, weights, limit


def attend(first, last, queries, kv_all):
    ctx_size, micro, _, span, padded = kv_all.shape
    row, kv, weights, limit = attention_specs(span, ctx_size)
    return pl.pallas_call(
        attend_kernel,
        grid=(micro, PAIRS // AT_ONCE),
        in_specs=[limit, limit, row, kv],
        out_specs=[row, weights],
        out_shape=[
            jax.ShapeDtypeStruct((micro, span, padded), jnp.bfloat16),
            jax.ShapeDtypeStruct((micro, 2 * PAIRS, span, ctx_size * span), jnp.bfloat16),
        ],
        compiler_params=pltpu.CompilerParams(vmem_limit_bytes=24 * 2**20),
    )(first, last, queries, kv_all)


def attend_back(queries, kv_all, grad, weights_all):
    ctx_size, micro, _, span, padded = kv_all.shape
    row, kv, weights, _ = attention_specs(span, ctx_size)
    return pl.pallas_call(
        attend_back_kernel,
        grid=(micro, PAIRS // AT_ONCE),
        in_specs=[row, kv, row, weights],
        out_specs=[row, kv],
        out_shape=[
            jax.ShapeDtypeStruct((micro, span, padded), jnp.bfloat16),
            jax.ShapeDtypeStruct(kv_all.shape, jnp.bfloat16),
        ],
        compiler_params=pltpu.CompilerParams(vmem_limit_bytes=24 * 2**20),
    )(queries, kv_all, grad, weights_all)


def padded_heads(rows, micro):
    rows = jnp.pad(rows, ((0, 0), (0, PAIRS * PAIR - rows.shape[1])))
    return rows.reshape(micro, -1, PAIRS * PAIR)


def plain_heads(rows, width):
    return rows.reshape(-1, rows.shape[-1])[:, :width]


def shared(block):
    count = lax.axis_size("dp")
    return [block] + [
        lax.ppermute(block, "dp", [(s, (s + k) % count) for s in range(count)])
        for k in range(1, count)
    ]


def returned(blocks):
    count = lax.axis_size("dp")
    total = blocks[0].astype(jnp.float32)
    for k in range(1, count):
        route = [(s, (s - k) % count) for s in range(count)]
        total = total + lax.ppermute(blocks[k], "dp", route).astype(jnp.float32)
    return total


def swapped(blocks, start, step):
    stacked = jnp.stack(blocks)
    count = len(blocks)
    return [
        lax.dynamic_index_in_dim(stacked, (start + step * j) % count, 0, keepdims=False)
        for j in range(count)
    ]


def dot32(left, right):
    return jnp.dot(left, right, preferred_element_type=jnp.float32)


def piece_route(k, dp_size, ctx_size):
    return [
        (d * ctx_size + r, r * dp_size + (d + k) % dp_size)
        for d in range(dp_size)
        for r in range(ctx_size)
    ]


def local(
    inputs,
    lengths,
    ln1_scale,
    ln1_bias,
    w_qkv,
    qv_bias,
    w_out,
    out_bias,
    ln2_scale,
    ln2_bias,
    w_up,
    up_bias,
    w_down,
    down_bias,
    out_grad,
):
    ctx_index = lax.axis_index("ctx")
    ctx_size = lax.axis_size("ctx")
    dp_index = lax.axis_index("dp")
    dp_size = lax.axis_size("dp")
    piece_index = (dp_index * ctx_size + ctx_index) % dp_size
    micro, _, span, width = inputs.shape
    rows = micro * span
    qkv_part = w_qkv.shape[1]
    out_part = w_out.shape[1]
    bf16 = jnp.bfloat16
    f32 = jnp.float32

    tokens32 = inputs.reshape(rows, width).astype(f32)
    grad_out = out_grad.reshape(rows, width)
    grad32 = grad_out.astype(f32)

    small = (ln1_scale, ln1_bias, qv_bias, out_bias, ln2_scale, ln2_bias, down_bias)
    small_all = lax.all_gather(jnp.concatenate(small), "dp", axis=0)
    vectors = []
    start = 0
    for member in small:
        size = member.shape[0]
        vectors.append(small_all[:, start : start + size].reshape(-1).astype(f32))
        start += size
    ln1_scale, ln1_bias, qv_bias, out_bias, ln2_scale, ln2_bias, down_bias = vectors
    lead = qkv_part // 256 * 128 or qkv_part // 2
    rest = qkv_part - lead
    lead_rows = lax.all_gather(w_qkv[:, :lead], "ctx", axis=0, tiled=True)
    rest_rows = jnp.concatenate(shared(w_qkv[:, lead:]), axis=1)
    lead_rows, rest_rows = lax.optimization_barrier((lead_rows, rest_rows))
    rest_near = lax.all_gather(rest_rows, "ctx", axis=0, tiled=True)
    lead_near = shared(lead_rows)
    out_near = shared(lax.all_gather(w_out, "ctx", axis=0, tiled=True))
    grad_all = jnp.concatenate(shared(grad_out), axis=0)
    up_here = lax.all_gather(w_up, "ctx", axis=0, tiled=True)
    down_rows = w_down.reshape(dp_size, -1, out_part)
    down_piece = [
        lax.ppermute(
            lax.dynamic_index_in_dim(down_rows, (dp_index + k) % dp_size, 0, keepdims=False),
            ("dp", "ctx"),
            piece_route(k, dp_size, ctx_size),
        )
        for k in range(dp_size)
    ]
    down_piece = jnp.concatenate(swapped(down_piece, piece_index, -1), axis=1)
    down_here = lax.all_gather(down_piece, "ctx", axis=0, tiled=True)

    normed1, normal1, inverse1 = layer_norm(tokens32, ln1_scale, ln1_bias)
    normed1 = normed1.astype(bf16)
    qkv_bias = jnp.concatenate([qv_bias[:width], jnp.zeros((width,), f32), qv_bias[width:]])
    rest_qkv = dot32(normed1, rest_near)
    qkv = [
        jnp.concatenate(
            [dot32(normed1, lead_near[k]), rest_qkv[:, k * rest : (k + 1) * rest]], axis=1
        )
        for k in range(dp_size)
    ]
    qkv = swapped(qkv, dp_index, -1)
    qkv = jnp.concatenate(qkv, axis=1)
    qkv = (qkv + qkv_bias).astype(bf16)
    queries = padded_heads(qkv[:, :width], micro)
    keys = padded_heads(qkv[:, width : 2 * width], micro)
    values = padded_heads(qkv[:, 2 * width :], micro)
    kv_all = lax.all_gather(jnp.stack([keys, values], axis=1), "ctx", axis=0)
    seq_ends = jnp.cumsum(lengths[:, 0], axis=1)
    last = ctx_index * span + jnp.arange(span, dtype=jnp.int32)
    last = jnp.broadcast_to(last[None, :, None], (micro, span, 1))
    ends = seq_ends[:, None, :]
    first = jnp.max(jnp.where(ends <= last, ends, 0), axis=2, keepdims=True).astype(jnp.int32)
    attended, weights = attend(first, last, queries, kv_all)
    attended = plain_heads(attended, width)
    branch = swapped([dot32(attended, piece) for piece in out_near], dp_index, -1)
    residual = tokens32 + jnp.concatenate(branch, axis=1) + out_bias
    normed2, normal2, inverse2 = layer_norm(residual, ln2_scale, ln2_bias)
    normed2_all = jnp.concatenate(shared(normed2.astype(bf16)), axis=0)

    gelu_input = dot32(normed2_all, up_here) + up_bias.astype(f32)
    hidden, gelu_pull = jax.vjp(jax.nn.gelu, gelu_input)
    hidden = hidden.astype(bf16)
    grad_upper = gelu_pull(back_dot(grad_all, down_here))[0].astype(bf16)
    both = jnp.concatenate(
        [dot32(hidden, down_here).astype(bf16), back_dot(grad_upper, up_here).astype(bf16)], axis=1
    )
    both = returned([both[k * rows : (k + 1) * rows] for k in range(dp_size)])
    up_grad = outer_sum(normed2_all, grad_upper).astype(bf16)
    down_grad = outer_sum(hidden, grad_all).astype(bf16)
    both, up_grad = lax.optimization_barrier((both, up_grad))
    block_out = (residual + both[:, :width] + down_bias).astype(bf16)
    grad_normed2 = both[:, width:]
    up_grad = lax.psum_scatter(up_grad.reshape(ctx_size, -1, up_here.shape[1]), "ctx")
    down_grad = lax.psum_scatter(down_grad.reshape(ctx_size, -1, width), "ctx")
    down_cols = [down_grad[:, j * out_part : (j + 1) * out_part] for j in range(dp_size)]
    down_cols = swapped(down_cols, piece_index, -1)
    down_grad = [
        lax.ppermute(
            down_cols[k], ("dp", "ctx"), [(b, a) for a, b in piece_route(k, dp_size, ctx_size)]
        )
        for k in range(dp_size)
    ]
    down_grad = jnp.concatenate(swapped(down_grad, -dp_index, 1), axis=0).astype(f32)

    grad_residual = grad32 + norm_back(grad_normed2, normal2, inverse2, ln2_scale)
    grad_branch = grad_residual.astype(bf16)
    branch_parts = [
        grad_branch[:, j * out_part : (j + 1) * out_part] for j in range(dp_size)
    ]
    branch_parts = swapped(branch_parts, dp_index, -1)
    grad_attended = back_dot(branch_parts[0], out_near[0])
    for k in range(1, dp_size):
        grad_attended = grad_attended + back_dot(branch_parts[k], out_near[k])
    grad_attended = padded_heads(grad_attended.astype(bf16), micro)
    out_grads = returned([outer_sum(attended, part).astype(bf16) for part in branch_parts])
    out_grads = out_grads.astype(bf16).reshape(ctx_size, -1, out_part)
    out_grads = lax.psum_scatter(out_grads, "ctx").astype(f32)
    grad_queries, grad_kv = attend_back(queries, kv_all, grad_attended, weights)
    grad_kv, up_grad = lax.optimization_barrier((grad_kv, up_grad))
    up_grad = up_grad.astype(f32)
    grad_kv = lax.psum_scatter(grad_kv, "ctx", scatter_dimension=0)
    grad_qkv = jnp.concatenate(
        [
            plain_heads(grad_queries, width),
            plain_heads(grad_kv[:, 0], width),
            plain_heads(grad_kv[:, 1], width),
        ],
        axis=1,
    )
    pieces = [grad_qkv[:, j * qkv_part : (j + 1) * qkv_part] for j in range(dp_size)]
    pieces = swapped(pieces, dp_index, -1)
    lead_pieces = [piece[:, :lead] for piece in pieces]
    rest_pieces = jnp.concatenate([piece[:, lead:] for piece in pieces], axis=1)
    qkv_grads = returned([outer_sum(normed1, piece).astype(bf16) for piece in pieces])
    grad_normed1 = back_dot(rest_pieces, rest_near)
    for k in range(dp_size):
        grad_normed1 = grad_normed1 + back_dot(lead_pieces[k], lead_near[k])
    input_grad = (grad_residual + norm_back(grad_normed1, normal1, inverse1, ln1_scale)).astype(
        bf16
    )

    qkv_sums = jnp.sum(grad_qkv.astype(f32), axis=0)
    sums = (
        jnp.sum(grad_normed1 * normal1, axis=0),
        jnp.sum(grad_normed1, axis=0),
        jnp.concatenate([qkv_sums[:width], qkv_sums[2 * width :]]),
        jnp.sum(grad_branch.astype(f32), axis=0),
        jnp.sum(grad_normed2 * normal2, axis=0),
        jnp.sum(grad_normed2, axis=0),
        jnp.sum(grad32, axis=0),
    )
    sums = jnp.concatenate([member.reshape(dp_size, -1) for member in sums], axis=1)
    sums = returned(swapped([sums[j] for j in range(dp_size)], dp_index, -1))
    up_sums = jnp.sum(grad_upper.astype(f32), axis=0)
    sums = jnp.concatenate([sums, up_sums]).reshape(-1, qkv_part)
    sums = jnp.pad(sums, ((0, 8 - sums.shape[0]), (0, 0)))
    sums = jnp.broadcast_to(sums[None], (ctx_size,) + sums.shape)
    qkv_rows = width // ctx_size
    qkv_grads = jnp.concatenate([qkv_grads.reshape(ctx_size, qkv_rows, qkv_part), sums], axis=1)
    qkv_grads = lax.psum_scatter(qkv_grads.astype(bf16), "ctx").astype(f32)
    sums = qkv_grads[qkv_rows:].reshape(-1)
    qkv_grads = qkv_grads[:qkv_rows]
    cuts = []
    start = 0
    for member in small + (up_bias,):
        cuts.append(sums[start : start + member.shape[0]])
        start += member.shape[0]
    return (
        block_out.reshape(inputs.shape),
        input_grad.reshape(inputs.shape),
        cuts[0],
        cuts[1],
        qkv_grads,
        cuts[2],
        out_grads,
        cuts[3],
        cuts[4],
        cuts[5],
        up_grad,
        cuts[7],
        down_grad,
        cuts[6],
    )


def solution(mesh):
    placed = (
        P(None, "dp", "ctx", None),
        P(None, "dp", None),
        P("dp"),
        P("dp"),
        P("ctx", "dp"),
        P("dp"),
        P("ctx", "dp"),
        P("dp"),
        P("dp"),
        P("dp"),
        P("ctx", "dp"),
        P("dp"),
        P("ctx", "dp"),
        P("dp"),
        P(None, "dp", "ctx", None),
    )
    return jax.shard_map(
        local,
        mesh=mesh,
        in_specs=placed,
        out_specs=(
            P(None, "dp", "ctx", None),
            P(None, "dp", "ctx", None),
            P("dp"),
            P("dp"),
            P("ctx", "dp"),
            P("dp"),
            P("ctx", "dp"),
            P("dp"),
            P("dp"),
            P("dp"),
            P("ctx", "dp"),
            P("dp"),
            P("ctx", "dp"),
            P("dp"),
        ),
        check_vma=False,
    )
```
